32 devices in a mesh: dp: 4 (over x, core), row: 4 (over z), col: 2 (over y).
Axes of the slice: x: 2, y: 2, z: 4, core: 2. Of those that a mesh axis runs over, the one named last changes fastest.
Arguments:
- x_in: bfloat16 [64, 197, 768], P(('dp', 'row'), None, 'col'), may hold values from -6 to 6
- cotangent: bfloat16 [64, 197, 768], P(('dp', 'row'), None, 'col'), may hold values from -6 to 6
- norm_gains: bfloat16 [2, 2, 768], P(None, None, 'col'), may hold values from 0.5 to 1.5
- norm_shifts: bfloat16 [2, 2, 768], P(None, None, 'col'), may hold values from -1.796875 to 1.796875
- w_qkv: bfloat16 [2, 3, 12, 64, 768], P(None, None, 'row', None, 'col'), may hold values from -0.21875 to 0.21875
- b_qkv: bfloat16 [2, 2, 12, 64], P(None, None, 'row'), may hold values from -3 to 3
- w_out: bfloat16 [2, 768, 768], P(None, 'row', 'col'), may hold values from -1.75 to 1.75
- out_biases: bfloat16 [2, 2, 768], P(None, None, 'col'), may hold values from -3 to 3
- w_up: bfloat16 [2, 768, 3072], P(None, 'col', 'row'), may hold values from -0.21875 to 0.21875
- b_up: bfloat16 [2, 3072], P(None, 'row'), may hold values from -3 to 3
- w_down: bfloat16 [2, 3072, 768], P(None, 'row', 'col'), may hold values from -0.109375 to 0.109375
Outputs:
- x_out: bfloat16 [64, 197, 768], P(('dp', 'row'), None, 'col')
- grad_input: float32 [64, 197, 768], P(('dp', 'row'), None, 'col')
- grad_norm_gains: float32 [2, 2, 768], P(None, None, 'col')
- grad_norm_shifts: float32 [2, 2, 768], P(None, None, 'col')
- grad_w_qkv: float32 [2, 3, 12, 64, 768], P(None, None, 'row', None, 'col')
- grad_b_qkv: float32 [2, 2, 12, 64], P(None, None, 'row')
- grad_w_out: float32 [2, 768, 768], P(None, 'row', 'col')
- grad_out_biases: float32 [2, 2, 768], P(None, None, 'col')
- grad_w_up: float32 [2, 768, 3072], P(None, 'col', 'row')
- grad_b_up: float32 [2, 3072], P(None, 'row')
- grad_w_down: float32 [2, 3072, 768], P(None, 'row', 'col')
The draws below stay inside these ranges and needn't reach their ends.
All inputs are finite; a program needn't handle non-finite values.
Results may differ from the reference program's by a relative error of at most 0.023.
Values may be sent and summed in bfloat16 or wider, within the bound.
A program may use at most 192 MiB of HBM per device.

```python
import jax
import jax.numpy as jnp
from jax import lax

D = 768
H = 12
HD = 64
FF = 3072
S = 197
LAYERS = 2
IMAGES = 64


def block_scale(own_key, dims, pieces, smallest, top_value):
    factor_of = 1.0
    for dim, parts in pieces:
        steps = jax.random.uniform(jax.random.fold_in(jax.random.fold_in(own_key, 6), dim), (parts,), jnp.float32, smallest / len(pieces), top_value / len(pieces))
        factor_of = factor_of * jnp.repeat(jnp.exp(steps), dims[dim] // parts).reshape((-1,) + (1,) * (len(dims) - 1 - dim))
    return factor_of


def bell_draw(key, shape, scale, bound, shards=(), held_as=jnp.bfloat16):
    entries = scale * jax.random.normal(key, shape, jnp.float32)
    if shards:
        entries = entries * block_scale(key, shape, shards, -0.22, 0.18)
    return jnp.clip(entries, -bound, bound).astype(held_as)


def setup_inputs(seed: int = 0) -> dict:
    splits = jax.random.split(jax.random.key(seed), 12)
    return {
        "x_in": bell_draw(splits[0], (IMAGES, S, D), 1.0, 6.0, ((0, 16), (2, 2))),
        "cotangent": bell_draw(splits[1], (IMAGES, S, D), 1.0, 6.0, ((0, 16), (2, 2))),
        "norm_gains": jnp.clip(1.0 + 0.1 * jax.random.normal(splits[2], (LAYERS, 2, D), jnp.float32), 0.5, 1.5).astype(jnp.bfloat16),
        "norm_shifts": bell_draw(splits[3], (LAYERS, 2, D), 0.3, 1.796875, ((2, 2),)),
        "w_qkv": bell_draw(splits[4], (LAYERS, 3, H, HD, D), D ** -0.5, 0.21875, ((2, 4), (4, 2))),
        "b_qkv": bell_draw(splits[5], (LAYERS, 2, H, HD), 0.5, 3.0, ((2, 4),)),
        "w_out": bell_draw(splits[6], (LAYERS, D, D), (max(D // 64, 1)) ** -0.5, 1.75, ((1, 4), (2, 2))),
        "out_biases": bell_draw(splits[7], (LAYERS, 2, D), 0.5, 3.0, ((2, 2),)),
        "w_up": bell_draw(splits[8], (LAYERS, D, FF), D ** -0.5, 0.21875, ((1, 2), (2, 4))),
        "b_up": bell_draw(splits[9], (LAYERS, FF), 0.5, 3.0, ((1, 4),)),
        "w_down": bell_draw(splits[10], (LAYERS, FF, D), FF ** -0.5, 0.109375, ((1, 4), (2, 2))),
    }


@jax.custom_vjp
def low(v):
    return lax.optimization_barrier(v.astype(jnp.bfloat16)).astype(jnp.float32)

@jax.custom_vjp
def low_back(v):
    return v

def low_keep(v):
    return (low(v), None)

def low_pass(kept, grad):
    return (grad,)

def back_keep(v):
    return (v, None)

def back_low(kept, grad):
    return (low(grad),)
low.defvjp(low_keep, low_pass)
low_back.defvjp(back_keep, back_low)
epsilon = 1e-06
highest = lax.Precision.HIGHEST

def normalize(stream, norm_gain, shift):
    centre = lax.optimization_barrier(jnp.mean(stream, axis=-1, keepdims=True))
    spread = lax.optimization_barrier(jnp.mean(stream * stream, axis=-1, keepdims=True)) - centre * centre
    return (stream - centre) * lax.rsqrt(spread + epsilon) * norm_gain + shift

def encoder_layer(stream, layer_params):
    norm_gain, shifts, weight_qkv, bias_qkv, weight_out, bias_pair, weight_up, bias_up, weight_down = layer_params
    normed = low(normalize(stream, norm_gain[0], shifts[0]))
    projected = jnp.einsum('bsd,thed->bsthe', normed, weight_qkv, precision=highest)
    bias_full = jnp.stack([bias_qkv[0], jnp.zeros_like(bias_qkv[0]), bias_qkv[1]])
    projected = low(low_back(projected + bias_full))
    query_h = projected[:, :, 0]
    key_h = projected[:, :, 1]
    value_h = projected[:, :, 2]
    scores = low_back(jnp.einsum('bqhe,bkhe->bhqk', query_h, key_h, precision=highest) * 0.125)
    prob_vals = low(jax.nn.softmax(scores, axis=-1))
    mixture = jnp.einsum('bhqk,bkhe->bqhe', prob_vals, value_h, precision=highest)
    mixture = low(low_back(mixture))
    mixture = mixture.reshape(mixture.shape[0], mixture.shape[1], H * HD)
    attended = low_back(jnp.dot(mixture, weight_out, precision=highest) + bias_pair[0])
    stream = stream + attended
    normed = low(normalize(stream, norm_gain[1], shifts[1]))
    hidden = low_back(jnp.dot(normed, weight_up, precision=highest) + bias_up)
    activated = low(jax.nn.gelu(hidden, approximate=False))
    branch = low_back(jnp.dot(activated, weight_down, precision=highest) + bias_pair[1])
    return stream + branch

def forward(stream, params):
    for layer_idx in range(LAYERS):
        stream = encoder_layer(stream, tuple((p[layer_idx] for p in params)))
    return stream

def reference(x_in, cotangent, norm_gains, norm_shifts, w_qkv, b_qkv, w_out, out_biases, w_up, b_up, w_down):
    params = tuple((p.astype(jnp.float32) for p in (norm_gains, norm_shifts, w_qkv, b_qkv, w_out, out_biases, w_up, b_up, w_down)))
    per_group = 16
    groups = x_in.shape[0] // per_group
    x_blocks = x_in.astype(jnp.float32).reshape(groups, per_group, S, D)
    cot_blocks = cotangent.astype(jnp.float32).reshape(groups, per_group, S, D)

    def scan_step(totals, item):
        x_block, cot_block = item
        output, pullback = jax.vjp(forward, x_block, params)
        d_input, d_params = pullback(cot_block)
        return (jax.tree.map(jnp.add, totals, d_params), (output.astype(jnp.bfloat16), d_input))
    zeros_tree = jax.tree.map(jnp.zeros_like, params)
    grads, (outputs, d_inputs) = lax.scan(scan_step, zeros_tree, (x_blocks, cot_blocks))
    return (outputs.reshape(x_in.shape), d_inputs.reshape(x_in.shape), grads[0], grads[1], grads[2], grads[3], grads[4], grads[5], grads[6], grads[7], grads[8])
```

```python
import functools

import jax
import jax.numpy as jnp
from jax import lax
from jax.sharding import PartitionSpec as P

HD = 64
LAYERS = 2
AXES = ("dp", "row", "col")
F32 = jnp.float32
BF16 = jnp.bfloat16


epsilon = 1e-06


def gelu_exact(values):
    return jax.nn.gelu(values, approximate=False)


def normalize(stream, norm_gain, shift):
    width = stream.shape[-1]
    centre = jnp.sum(stream, axis=-1, keepdims=True) / width
    spread = jnp.sum(stream * stream, axis=-1, keepdims=True) / width - centre * centre
    inv_scale = lax.rsqrt(spread + epsilon)
    unit_vals = (stream - centre) * inv_scale
    normed = (unit_vals * norm_gain + shift).astype(BF16)
    return normed, unit_vals, inv_scale


def normalize_back(d_normed, unit_vals, inv_scale, norm_gain):
    width = d_normed.shape[-1]
    d_gain = jnp.sum(d_normed * unit_vals, axis=0)
    d_shift = jnp.sum(d_normed, axis=0)
    d_unit = d_normed * norm_gain
    sum_one = jnp.sum(d_unit, axis=-1, keepdims=True)
    sum_two = jnp.sum(d_unit * unit_vals, axis=-1, keepdims=True)
    d_input = inv_scale * (d_unit - sum_one / width - unit_vals * (sum_two / width))
    return d_input, d_gain, d_shift


def matmul(spec, left, right):
    return jnp.einsum(spec, left, right, preferred_element_type=F32)


def shards(
    sizes,
    x_in,
    cotangent,
    norm_gains,
    norm_shifts,
    w_qkv,
    b_qkv,
    w_out,
    out_biases,
    w_up,
    b_up,
    w_down,
):
    n_dp, n_row, n_col = sizes
    my_dp = lax.axis_index("dp")
    my_row = lax.axis_index("row")
    my_col = lax.axis_index("col")
    heads_local = w_qkv.shape[2]
    heads = heads_local * n_row
    wide = x_in.shape[-1]
    width = wide * n_col
    part_e = HD // n_dp
    part_m = w_out.shape[1] // n_dp
    part_f = w_down.shape[1] // n_dp
    rows_qkv = 3 * heads_local * part_e
    hidden_units = w_down.shape[1] * n_row

    def part(values, size, axis):
        return lax.dynamic_slice_in_dim(values, my_dp * size, size, axis)

    small = jnp.concatenate(
        [
            norm_gains.reshape(-1, wide),
            norm_shifts.reshape(-1, wide),
            out_biases.reshape(-1, wide),
        ]
    )
    small_rows = jnp.concatenate([b_qkv.reshape(-1), b_up.reshape(-1)])
    n_small = small.shape[0]
    n_side = -(-small_rows.shape[0] // wide)
    side_pad = n_side * wide - small_rows.shape[0]
    small_rows = jnp.pad(small_rows, (0, side_pad)).reshape(n_side, wide)

    def gather_attn(layer):
        pieces = [
            part(w_qkv[layer], part_e, 2).reshape(rows_qkv, wide),
            part(w_out[layer], part_m, 0),
        ]
        if layer == 0:
            pieces += [small, small_rows]
        packed = jnp.concatenate(pieces)
        got = lax.all_gather(packed, AXES, axis=0, tiled=False)
        return got.reshape(n_dp, n_row, n_col, -1, wide)

    def gather_ff(layer):
        packed = jnp.concatenate(
            [part(w_up[layer].T, part_f, 0), part(w_down[layer], part_f, 0)]
        )
        got = lax.all_gather(packed, AXES, axis=0, tiled=False)
        return got.reshape(n_dp, n_row, n_col, -1, wide)

    def whole_rows(got):
        return got.transpose(1, 0, 3, 2, 4).reshape(-1, width)

    def whole_qkv(got):
        got = got.reshape(n_dp, n_row, n_col, 3, heads_local, part_e, wide)
        return got.transpose(3, 1, 4, 0, 5, 2, 6).reshape(3, heads * HD, width)

    def cut_rows(grad, size):
        grad = grad.astype(BF16).reshape(n_row, n_dp, size, n_col, wide)
        return grad.transpose(1, 0, 3, 2, 4).reshape(-1, size, wide)

    def cut_qkv(grad):
        grad = grad.astype(BF16).reshape(3, n_row, heads_local, n_dp, part_e, n_col, wide)
        return grad.transpose(3, 1, 5, 0, 2, 4, 6).reshape(-1, rows_qkv, wide)

    def spread_sum(cuts):
        packed = jnp.concatenate(cuts, axis=1)
        return lax.psum_scatter(packed, AXES, scatter_dimension=0, tiled=False)

    tokens = x_in.shape[1]
    padded = -(-tokens // 16) * 16

    def to_images(values):
        both = lax.all_to_all(values, "col", split_axis=1, concat_axis=3, tiled=True)
        return jnp.pad(both, ((0, 0), (0, 0), (0, padded - tokens), (0, 0)))

    def to_blocks(values):
        values = values.astype(BF16).reshape(-1, padded, width)[:, :tokens]
        return lax.all_to_all(values, "col", split_axis=2, concat_axis=0, tiled=True)

    got_attn = [gather_attn(layer) for layer in range(LAYERS)]
    got_ff = [gather_ff(layer) for layer in range(LAYERS)]
    streams = to_images(jnp.stack([x_in, cotangent]))
    images = streams.shape[1]
    stream = streams[0].reshape(-1, width).astype(F32)

    cut_a = rows_qkv + part_m
    got_small = got_attn[0][0, 0, :, cut_a : cut_a + n_small]
    got_small = got_small.transpose(1, 0, 2).reshape(3, LAYERS, 2, width).astype(F32)
    gains, shifts, biases = got_small[0], got_small[1], got_small[2]
    got_side = got_attn[0][0, :, 0, cut_a + n_small :].reshape(n_row, -1)
    n_bqkv = b_qkv.size
    bias_qkv = got_side[:, :n_bqkv].reshape(n_row, LAYERS, 2, heads_local * HD)
    bias_qkv = bias_qkv.transpose(1, 2, 0, 3).reshape(LAYERS, 2, heads * HD).astype(F32)
    bias_up = got_side[:, n_bqkv : n_bqkv + b_up.size].reshape(n_row, LAYERS, -1)
    bias_up = bias_up.transpose(1, 0, 2).reshape(LAYERS, hidden_units).astype(F32)

    key_mask = jnp.arange(padded) < tokens

    def split_heads(values):
        return values.reshape(images, padded, heads, HD).transpose(0, 2, 1, 3)

    def join_heads(values):
        return values.transpose(0, 2, 1, 3).reshape(images * padded, heads * HD)

    kept_values = []
    for layer in range(LAYERS):
        weight_qkv = whole_qkv(got_attn[layer][..., :rows_qkv, :])
        weight_out = whole_rows(got_attn[layer][..., rows_qkv:cut_a, :])
        normed_a, unit_a, scale_a = normalize(stream, gains[layer, 0], shifts[layer, 0])
        query_h = matmul("td,kd->tk", normed_a, weight_qkv[0]) + bias_qkv[layer, 0]
        key_h = matmul("td,kd->tk", normed_a, weight_qkv[1])
        value_h = matmul("td,kd->tk", normed_a, weight_qkv[2]) + bias_qkv[layer, 1]
        query_h, key_h, value_h = (
            split_heads(v.astype(BF16)) for v in (query_h, key_h, value_h)
        )
        scores = matmul("bhqe,bhke->bhqk", query_h, key_h) * 0.125
        scores = jnp.where(key_mask, scores, -jnp.inf)
        row_max = jnp.max(scores, axis=-1, keepdims=True)
        exp_vals = jnp.exp(scores - row_max)
        probs = exp_vals / jnp.sum(exp_vals, axis=-1, keepdims=True)
        mixture = join_heads(
            matmul("bhqk,bhke->bhqe", probs.astype(BF16), value_h).astype(BF16)
        )
        stream = stream + (matmul("tm,md->td", mixture, weight_out) + biases[layer, 0])
        normed_b, unit_b, scale_b = normalize(stream, gains[layer, 1], shifts[layer, 1])
        weight_up = whole_rows(got_ff[layer][..., :part_f, :])
        weight_down = whole_rows(got_ff[layer][..., part_f:, :])
        hidden = matmul("td,fd->tf", normed_b, weight_up) + bias_up[layer]
        activated = gelu_exact(hidden).astype(BF16)
        stream = stream + (matmul("tf,fd->td", activated, weight_down) + biases[layer, 1])
        kept_values.append(
            (
                (weight_qkv, weight_out, weight_up, weight_down),
                (normed_a, unit_a, scale_a),
                (query_h, key_h, value_h, probs, mixture),
                (normed_b, unit_b, scale_b),
                (hidden, activated),
            )
        )

    result = to_blocks(stream)
    d_stream = streams[1].reshape(-1, width).astype(F32)
    small_grads = [None] * LAYERS
    sums_attn = [None] * LAYERS
    sums_ff = [None] * LAYERS
    for layer in reversed(range(LAYERS)):
        weights, norm_a, attn, norm_b, ff = kept_values[layer]
        weight_qkv, weight_out, weight_up, weight_down = weights
        normed_a, unit_a, scale_a = norm_a
        query_h, key_h, value_h, probs, mixture = attn
        normed_b, unit_b, scale_b = norm_b
        hidden, activated = ff
        d_rows = d_stream.astype(BF16)
        d_bias_down = jnp.sum(d_rows, axis=0, dtype=F32)
        d_w_down = matmul("tf,td->fd", activated, d_rows)
        d_activated = matmul("td,fd->tf", d_rows, weight_down)
        d_hidden = jax.vjp(gelu_exact, hidden)[1](d_activated)[0].astype(BF16)
        d_b_up = jnp.sum(d_hidden, axis=0, dtype=F32)
        d_w_up = matmul("tf,td->fd", d_hidden, normed_b)
        sums_ff[layer] = spread_sum([cut_rows(d_w_up, part_f), cut_rows(d_w_down, part_f)])
        d_normed = matmul("tf,fd->td", d_hidden, weight_up)
        d_input, d_gain_b, d_shift_b = normalize_back(d_normed, unit_b, scale_b, gains[layer, 1])
        d_stream = d_stream + d_input
        d_rows = d_stream.astype(BF16)
        d_bias_out = jnp.sum(d_rows, axis=0, dtype=F32)
        d_w_out = matmul("tm,td->md", mixture, d_rows)
        d_mix = split_heads(matmul("td,md->tm", d_rows, weight_out).astype(BF16))
        d_value = matmul("bhqk,bhqe->bhke", probs.astype(BF16), d_mix)
        d_probs = matmul("bhqe,bhke->bhqk", d_mix, value_h)
        d_scores = (
            probs * (d_probs - jnp.sum(probs * d_probs, axis=-1, keepdims=True))
        ).astype(BF16)
        d_query = matmul("bhqk,bhke->bhqe", d_scores, key_h) * 0.125
        d_key = matmul("bhqk,bhqe->bhke", d_scores, query_h) * 0.125
        d_query, d_key, d_value = (
            join_heads(v.astype(BF16)) for v in (d_query, d_key, d_value)
        )
        d_b_qkv = jnp.stack(
            [jnp.sum(d_query, axis=0, dtype=F32), jnp.sum(d_value, axis=0, dtype=F32)]
        )
        d_w_qkv = jnp.stack(
            [matmul("tk,td->kd", v, normed_a) for v in (d_query, d_key, d_value)]
        )
        sums_attn[layer] = spread_sum([cut_qkv(d_w_qkv), cut_rows(d_w_out, part_m)])
        d_normed = (
            matmul("tk,kd->td", d_query, weight_qkv[0])
            + matmul("tk,kd->td", d_key, weight_qkv[1])
            + matmul("tk,kd->td", d_value, weight_qkv[2])
        )
        d_input, d_gain_a, d_shift_a = normalize_back(d_normed, unit_a, scale_a, gains[layer, 0])
        d_stream = d_stream + d_input
        small_grads[layer] = (
            jnp.stack([d_gain_a, d_gain_b]),
            jnp.stack([d_shift_a, d_shift_b]),
            jnp.stack([d_bias_out, d_bias_down]),
            d_b_qkv,
            d_b_up,
        )

    stacked = [jnp.stack([small_grads[layer][m] for layer in range(LAYERS)]) for m in range(5)]
    summed = lax.psum(jnp.concatenate([s.reshape(-1) for s in stacked]), AXES)
    ends = []
    start = 0
    for member in stacked:
        ends.append(summed[start : start + member.size].reshape(member.shape))
        start += member.size

    def my_cols(values):
        return lax.dynamic_slice_in_dim(values, my_col * wide, wide, 2)

    def my_rows(values):
        size = values.shape[-1] // n_row
        return lax.dynamic_slice_in_dim(values, my_row * size, size, values.ndim - 1)

    gains_grad, shifts_grad, biases_grad = (my_cols(v) for v in ends[:3])
    b_qkv_grad = my_rows(ends[3]).reshape(b_qkv.shape)
    b_up_grad = my_rows(ends[4])

    def over_dp(values):
        return lax.all_gather(values, "dp", axis=0, tiled=False)

    out_qkv, out_out, out_up, out_down = [], [], [], []
    for layer in range(LAYERS):
        attn_sum = over_dp(sums_attn[layer]).astype(F32)
        ff_sum = over_dp(sums_ff[layer]).astype(F32)
        qkv_sum = attn_sum[:, :rows_qkv].reshape(n_dp, 3, heads_local, part_e, wide)
        out_qkv.append(qkv_sum.transpose(1, 2, 0, 3, 4).reshape(w_qkv.shape[1:]))
        out_out.append(attn_sum[:, rows_qkv:].reshape(-1, wide))
        out_up.append(ff_sum[:, :part_f].reshape(-1, wide).T)
        out_down.append(ff_sum[:, part_f:].reshape(-1, wide))

    return (
        result,
        to_blocks(d_stream).astype(F32),
        gains_grad,
        shifts_grad,
        jnp.stack(out_qkv),
        b_qkv_grad,
        jnp.stack(out_out),
        biases_grad,
        jnp.stack(out_up),
        b_up_grad,
        jnp.stack(out_down),
    )


def solution(mesh):
    sizes = tuple(mesh.shape[axis] for axis in AXES)
    return jax.shard_map(
        functools.partial(shards, sizes),
        mesh=mesh,
        in_specs=(
            P(("dp", "row"), None, "col"),
            P(("dp", "row"), None, "col"),
            P(None, None, "col"),
            P(None, None, "col"),
            P(None, None, "row", None, "col"),
            P(None, None, "row", None),
            P(None, "row", "col"),
            P(None, None, "col"),
            P(None, "col", "row"),
            P(None, "row"),
            P(None, "row", "col"),
        ),
        out_specs=(
            P(("dp", "row"), None, "col"),
            P(("dp", "row"), None, "col"),
            P(None, None, "col"),
            P(None, None, "col"),
            P(None, None, "row", None, "col"),
            P(None, None, "row", None),
            P(None, "row", "col"),
            P(None, None, "col"),
            P(None, "col", "row"),
            P(None, "row"),
            P(None, "row", "col"),
        ),
        check_vma=False,
    )
```
